32 devices in a mesh: hyper: 2 (over y), row: 16 (over z, x, core).
Axes of the slice: x: 2, y: 2, z: 4, core: 2. Of those that a mesh axis runs over, the one named last changes fastest.
Arguments:
- top_sigma: bfloat16 [20480, 10240], P(('hyper', 'row')), parts along dimension 0, may hold values from -1 to 5
- parent_pattern: int32 [16, 4], replicated, may hold values from 0 to 39, as said below
- parent_panel: bfloat16 [32, 1024, 256], P(('hyper', 'row')), parts along dimension 0, may hold values from -0.375 to 0.375
- parent_inverse: bfloat16 [32, 256, 256], P(('hyper', 'row')), parts along dimension 0, may hold values from -1 to 5
- child_pattern: int32 [128, 2], P('row'), may hold values from 0 to 3, as said below
- child_panel: bfloat16 [256, 768, 256], P(('hyper', 'row')), parts along dimension 0, may hold values from -0.375 to 0.375
- child_inverse: bfloat16 [256, 256, 256], P(('hyper', 'row')), parts along dimension 0, may hold values from -1 to 5
- child_count: int32 [16], P('row'), may hold values from 1 to 8
Outputs:
- parent_column: bfloat16 [32, 1024, 256], P(('hyper', 'row')), parts along dimension 0
- parent_block: float32 [32, 256, 256], P(('hyper', 'row')), parts along dimension 0
- child_column: bfloat16 [256, 768, 256], P(('hyper', 'row')), parts along dimension 0
- child_block: float32 [256, 256, 256], P(('hyper', 'row')), parts along dimension 0
The draws below stay inside these ranges and needn't reach their ends.
There are 2 independent parts, one for each index of `hyper`. The reference program is written for one: setup_inputs(seed, part) draws one part's arguments, and reference() takes and returns one part's arrays. A program takes and returns all parts, laid end to end along the dimension named above; an argument that names none is the same for every part. Nothing has to cross between parts.
Inputs may be any that keep to these rules, and one draw needn't show every extreme that they name: `parent_pattern`: each row names 4 distinct supernodes in increasing order. `child_pattern`: each row names 2 distinct positions in increasing order.
All inputs are finite; a program needn't handle non-finite values.
Results may differ from the reference program's by a relative error of at most 0.005.
Values may be sent and summed in bfloat16 or wider, within the bound.
A program may use at most 192 MiB of HBM per device.

```python
import jax
import jax.numpy as jnp
from jax import lax

SUPER = 256
TOP = 40
STRUCT_A = 4
STRUCT_B = 2
KIDS = 8
PARENTS = 16
CHILDREN = 128
N_ROW = 16


def symmetric_blocks(key, number, width, offscale, lowest, highest):
    key_noise, key_diag = jax.random.split(key)
    noise = jax.random.normal(key_noise, (number, width, width), jnp.float32) * offscale
    noise = 0.5 * (noise + jnp.swapaxes(noise, 1, 2))
    diagonal = jax.random.uniform(key_diag, (number, width), jnp.float32, lowest, highest)
    return noise + diagonal[:, :, None] * jnp.eye(width, dtype=jnp.float32)[None]


def draw_top_sigma(key, part):
    key = jax.random.fold_in(key, 3)
    values = symmetric_blocks(key, 1, TOP * SUPER, 0.02, 0.5, 2.0)
    return values[0].astype(jnp.bfloat16)


def draw_parent_inverse(key, part):
    key = jax.random.fold_in(key, 5)
    values = symmetric_blocks(key, N_ROW, SUPER, 0.03, 0.5, 2.0)
    return values.astype(jnp.bfloat16)


def draw_child_inverse(key, part):
    key = jax.random.fold_in(key, 7)
    values = symmetric_blocks(key, KIDS * N_ROW, SUPER, 0.03, 0.5, 2.0)
    return values.astype(jnp.bfloat16)


def sorted_subsets(key, rows, universe, picks):
    keys = jax.random.split(key, rows)
    chosen = jax.vmap(lambda single: jnp.sort(jax.random.permutation(single, universe)[:picks]))(keys)
    spread = jnp.arange(picks, dtype=jnp.int32) * (universe - 1) // (picks - 1)
    return chosen.at[0].set(spread).astype(jnp.int32)


def draw_parent_pattern(key, part):
    key = jax.random.fold_in(key, 11)
    return sorted_subsets(key, N_ROW, TOP, STRUCT_A)


def draw_child_pattern(key, part):
    key = jax.random.fold_in(key, 13)
    return sorted_subsets(key, KIDS * N_ROW, STRUCT_A, STRUCT_B)


def draw_child_count(key, part):
    key = jax.random.fold_in(key, 17)
    counts = jax.random.randint(key, (N_ROW,), 1, KIDS + 1, dtype=jnp.int32)
    counts = counts.at[0].set(KIDS)
    counts = counts.at[1].set(1)
    return counts.astype(jnp.int32)


def block_levels(key, dims, cuts, least, largest):
    gain = 1.0
    for dim, parts in cuts:
        heights = jax.random.uniform(jax.random.fold_in(jax.random.fold_in(key, 6), dim), (parts,), jnp.float32, least / len(cuts), largest / len(cuts))
        gain = gain * jnp.repeat(jnp.exp(heights), dims[dim] // parts).reshape((-1,) + (1,) * (len(dims) - 1 - dim))
    return gain


def normal_values(key, shape, scale, most, pieces=(), kind=jnp.bfloat16):
    drawn = scale * jax.random.normal(key, shape, jnp.float32)
    if pieces:
        drawn = drawn * block_levels(key, shape, pieces, -0.22, 0.18)
    return jnp.clip(drawn, -most, most).astype(kind)


def setup_inputs(seed: int = 0, part: int = 0) -> dict:
    splits = jax.random.split(jax.random.key(seed), 9)
    part_splits = jax.random.split(jax.random.fold_in(splits[8], part), 9)
    top_sigma = draw_top_sigma(jax.random.fold_in(jax.random.fold_in(splits[8], part), 71), part)
    parent_pattern = draw_parent_pattern(jax.random.fold_in(splits[8], 71), part)
    parent_panel = normal_values(part_splits[2], (PARENTS, STRUCT_A * SUPER, SUPER), SUPER ** -0.5, 0.375, ((0, 16),))
    parent_inverse = draw_parent_inverse(jax.random.fold_in(jax.random.fold_in(splits[8], part), 71), part)
    child_pattern = draw_child_pattern(jax.random.fold_in(splits[8], 71), part)
    child_panel = normal_values(part_splits[5], (CHILDREN, (1 + STRUCT_B) * SUPER, SUPER), SUPER ** -0.5, 0.375, ((0, 16),))
    child_inverse = draw_child_inverse(jax.random.fold_in(jax.random.fold_in(splits[8], part), 71), part)
    child_count = draw_child_count(jax.random.fold_in(splits[8], 71), part)
    return {"top_sigma": top_sigma, "parent_pattern": parent_pattern, "parent_panel": parent_panel, "parent_inverse": parent_inverse, "child_pattern": child_pattern, "child_panel": child_panel, "child_inverse": child_inverse, "child_count": child_count}


def assemble(parent_half, parent_col, sigma_local, positions, supernode):
    pick_count = positions.shape[0]
    struct_len = parent_col.shape[0] // supernode
    ss_blocks = sigma_local.reshape(struct_len, supernode, struct_len, supernode)
    chosen = jnp.take(jnp.take(ss_blocks, positions, axis=0), positions, axis=2)
    chosen = chosen.reshape(pick_count * supernode, pick_count * supernode)
    beside = jnp.take(parent_col.reshape(struct_len, supernode, supernode), positions, axis=0)
    beside = beside.reshape(pick_count * supernode, supernode)
    upper_row = jnp.concatenate([parent_half, beside.T], axis=1)
    lower_row = jnp.concatenate([beside, chosen], axis=1)
    return jnp.concatenate([upper_row, lower_row], axis=0)


def reference(top_sigma, parent_pattern, parent_panel, parent_inverse, child_pattern, child_panel, child_inverse, child_count):
    supernode = parent_inverse.shape[-1]
    top_blocks = top_sigma.shape[0] // supernode
    blocks_four = top_sigma.reshape(top_blocks, supernode, top_blocks, supernode)

    def one_parent(index):
        pattern = parent_pattern[index]
        width_all = pattern.shape[0] * supernode
        sigma_local = jnp.take(jnp.take(blocks_four, pattern, axis=0), pattern, axis=2).reshape(width_all, width_all)
        product = jnp.dot(sigma_local, parent_panel[index], preferred_element_type=jnp.float32)
        column = (-product).astype(jnp.bfloat16)
        diagonal = parent_inverse[index].astype(jnp.float32) - jnp.dot(parent_panel[index].T, column, preferred_element_type=jnp.float32)
        return sigma_local, column, diagonal

    locals_all, columns, diagonals = lax.map(one_parent, jnp.arange(parent_pattern.shape[0], dtype=jnp.int32))
    halves = diagonals.astype(jnp.bfloat16)

    def one_child(index):
        device = index // KIDS
        parent = jnp.bitwise_xor(device, 1)
        live = (index % KIDS) < child_count[device]
        matrix = assemble(halves[parent], columns[parent], locals_all[parent], child_pattern[index], supernode)
        product = jnp.dot(matrix, child_panel[index], preferred_element_type=jnp.float32)
        column = (-product).astype(jnp.bfloat16)
        diagonal = child_inverse[index].astype(jnp.float32) - jnp.dot(child_panel[index].T, column, preferred_element_type=jnp.float32)
        column = jnp.where(live, column, jnp.zeros_like(column))
        diagonal = jnp.where(live, diagonal, jnp.zeros_like(diagonal))
        return column, diagonal

    child_col, child_diag = lax.map(one_child, jnp.arange(child_pattern.shape[0], dtype=jnp.int32))
    return columns, diagonals, child_col, child_diag
```

```python
import functools
import math

import jax
import jax.numpy as jnp
from jax import lax
from jax.experimental import pallas as pl
from jax.experimental.pallas import tpu as pltpu
from jax.sharding import PartitionSpec as P

BF16 = jnp.bfloat16
F32 = jnp.float32
VMEM_LIMIT = 40 * 2**20


def swapped(value, axis, distance):
    mask = 2**distance
    pairs = [(source, source ^ mask) for source in range(lax.axis_size(axis))]
    return lax.ppermute(value, axis, pairs)


def dot(a, b):
    return jnp.dot(a, b, preferred_element_type=F32)


def dot_t(a, b):
    return lax.dot_general(a, b, (((0,), (0,)), ((), ())), preferred_element_type=F32)


def pack_kernel(items, per_parent, struct, super_, groups, own, offset, rank, pattern, top, out, sem):
    def copies(item):
        parent = item // per_parent
        for c in range(struct):
            column = pl.multiple_of(pattern[parent, c] * super_, super_)
            yield pltpu.make_async_copy(
                top.at[pl.ds(offset[item] * groups, groups), :, pl.ds(column, super_)],
                out.at[:, c, rank[item]],
                sem,
            )

    def mine(item):
        return jnp.logical_and(offset[item] >= 0, offset[item] < own)

    @pl.loop(0, items)
    def _(item):
        @pl.when(mine(item))
        def _():
            for copy in copies(item):
                copy.start()

    @pl.loop(0, items)
    def _(item):
        @pl.when(mine(item))
        def _():
            for copy in copies(item):
                copy.wait()


def pick_kernel(items, per_parent, source, rank, held, out, sem):
    @pl.loop(0, items)
    def _(item):
        pltpu.make_async_copy(
            held.at[source[item], rank[item]],
            out.at[item // per_parent, lax.rem(item, per_parent)],
            sem,
        ).start()

    pltpu.make_async_copy(out, out, sem).wait()


def sigma_block(raw, a, c):
    groups, _, _, halves = raw.shape[:4]
    return jnp.concatenate(
        [raw[i, c, a, h] for h in range(halves) for i in range(groups)], axis=0
    )


def parent_kernel(raw, panel, inverse, column, diagonal, both):
    struct = raw.shape[1]
    width = inverse.shape[-1]
    total = inverse[0].astype(F32)
    for a in range(struct):
        product = jnp.zeros((width, width), F32)
        for c in range(struct):
            product += dot(sigma_block(raw, a, c), panel[0, pl.ds(c * width, width), :])
        col = (-product).astype(BF16)
        column[0, pl.ds(a * width, width), :] = col
        both[a] = col
        total -= dot_t(panel[0, pl.ds(a * width, width), :], col)
    diagonal[0] = total
    both[struct] = total.astype(BF16)


def child_kernel(positions, count, raw, both, panel, inverse, column, diagonal, sigma, beside_t):
    struct = raw.shape[1]
    width = inverse.shape[-1]
    picks = positions.shape[1]
    child = pl.program_id(0)

    @pl.when(child == 0)
    def _():
        for a in range(struct):
            for c in range(struct):
                sigma[a * struct + c] = sigma_block(raw, a, c)
            beside_t[a] = both[a].T

    @pl.when(child < count[0])
    def _():
        q = [positions[child, i] for i in range(picks)]
        parts = [panel[0, pl.ds(i * width, width), :] for i in range(picks + 1)]
        product = dot(both[struct], parts[0])
        for i in range(picks):
            product += dot(beside_t[q[i]], parts[1 + i])
        col = (-product).astype(BF16)
        column[0, pl.ds(0, width), :] = col
        total = inverse[0].astype(F32) - dot_t(parts[0], col)
        for i in range(picks):
            product = dot(both[q[i]], parts[0])
            for j in range(picks):
                product += dot(sigma[q[i] * struct + q[j]], parts[1 + j])
            col = (-product).astype(BF16)
            column[0, pl.ds((1 + i) * width, width), :] = col
            total -= dot_t(parts[1 + i], col)
        diagonal[0] = total

    @pl.when(child >= count[0])
    def _():
        column[...] = jnp.zeros_like(column)
        diagonal[...] = jnp.zeros_like(diagonal)


def parent_solve(raw, panel, inverse):
    struct, width = raw.shape[1], inverse.shape[-1]
    return pl.pallas_call(
        parent_kernel,
        out_shape=(
            jax.ShapeDtypeStruct((1, struct * width, width), BF16),
            jax.ShapeDtypeStruct((1, width, width), F32),
            jax.ShapeDtypeStruct((struct + 1, width, width), BF16),
        ),
        compiler_params=pltpu.CompilerParams(vmem_limit_bytes=VMEM_LIMIT),
        name="parent",
    )(raw, panel, inverse)


def children_solve(raw, both, positions, panel, inverse, count):
    kids, rows, width = panel.shape
    struct = raw.shape[1]

    def whole(shape):
        return pl.BlockSpec(shape, lambda k, *_: (0,) * len(shape))

    def one(shape):
        return pl.BlockSpec((1,) + shape, lambda k, *_: (k, 0, 0))

    return pl.pallas_call(
        child_kernel,
        grid_spec=pltpu.PrefetchScalarGridSpec(
            num_scalar_prefetch=2,
            grid=(kids,),
            in_specs=[whole(raw.shape), whole(both.shape), one((rows, width)), one((width, width))],
            out_specs=[one((rows, width)), one((width, width))],
            scratch_shapes=[
                pltpu.VMEM((struct * struct, width, width), BF16),
                pltpu.VMEM((struct, width, width), BF16),
            ],
        ),
        out_shape=(
            jax.ShapeDtypeStruct((kids, rows, width), BF16),
            jax.ShapeDtypeStruct((kids, width, width), F32),
        ),
        compiler_params=pltpu.CompilerParams(vmem_limit_bytes=VMEM_LIMIT),
        name="children",
    )(positions, count, raw, both, panel, inverse)


def exchange_plain(top_sigma, parent_pattern, width):
    devices = parent_pattern.shape[0]
    strip, total_rows = top_sigma.shape
    struct = parent_pattern.shape[1]
    blocks = total_rows // width
    picked = jnp.take(top_sigma.reshape(strip, blocks, width), parent_pattern, axis=1)
    outgoing = jnp.transpose(picked, (1, 0, 2, 3)).reshape(devices, strip, struct * width)
    arrived = lax.all_to_all(outgoing, "row", split_axis=0, concat_axis=1, tiled=True)
    columns = arrived[0].reshape(blocks, width, struct, width)
    mine = jnp.take(columns, parent_pattern[lax.axis_index("row")], axis=0)
    return jnp.transpose(mine, (2, 0, 1, 3))[None, :, :, None]


def schedule(parent_pattern, halves, own):
    units = (parent_pattern[:, :, None] * halves + jnp.arange(halves, dtype=jnp.int32)).reshape(-1)
    source = units // own
    earlier = jnp.arange(units.size)[None, :] < jnp.arange(units.size)[:, None]
    rank = jnp.sum(
        jnp.logical_and(source[None, :] == source[:, None], earlier), axis=1, dtype=jnp.int32
    )
    offset = units - lax.axis_index("row") * own
    return source, offset, rank


def exchange_two_hops(top_sigma, parent_pattern, width, unit, groups):
    devices, struct = parent_pattern.shape
    halves, own = width // unit, top_sigma.shape[0] // unit
    per_parent = struct * halves
    items = devices * per_parent
    piece = unit // groups
    source, offset, rank = schedule(parent_pattern, halves, own)
    most = devices * min(own, per_parent)
    levels = [k for k in (12, 13, 14, 15, 16, 17, 18, 20, 24, 32, 48) if k < most] + [most]
    strips = top_sigma.reshape(top_sigma.shape[0] // piece, piece, top_sigma.shape[1])
    smem = pl.BlockSpec(memory_space=pltpu.SMEM)
    hbm = pl.BlockSpec(memory_space=pl.ANY)

    def hop(slots, strips, source, offset, rank, pattern):
        outgoing = pl.pallas_call(
            functools.partial(pack_kernel, items, per_parent, struct, width, groups, own),
            out_shape=jax.ShapeDtypeStruct((groups, struct, slots, piece, width), BF16),
            in_specs=[smem, smem, smem, hbm],
            out_specs=hbm,
            scratch_shapes=[pltpu.SemaphoreType.DMA],
            name="pack",
        )(offset, rank, pattern, strips)
        outgoing = outgoing.reshape(devices, slots, piece, width)
        held = lax.all_to_all(outgoing, "row", split_axis=0, concat_axis=0, tiled=True)
        return pl.pallas_call(
            functools.partial(pick_kernel, items, per_parent),
            out_shape=jax.ShapeDtypeStruct((devices, per_parent, piece, width), BF16),
            in_specs=[smem, smem, hbm],
            out_specs=hbm,
            scratch_shapes=[pltpu.SemaphoreType.DMA],
            name="pick",
        )(source, rank, held)

    needed = jnp.max(rank) + 1
    level = jnp.sum(needed > jnp.array(levels[:-1], jnp.int32), dtype=jnp.int32)
    outgoing = lax.switch(
        level,
        [functools.partial(hop, slots) for slots in levels],
        strips, source, offset, rank, parent_pattern,
    )
    arrived = lax.all_to_all(outgoing, "row", split_axis=0, concat_axis=0, tiled=True)
    return arrived.reshape(groups, struct, struct, halves, piece, width)


def local(
    top_sigma,
    parent_pattern,
    parent_panel,
    parent_inverse,
    child_pattern,
    child_panel,
    child_inverse,
    child_count,
):
    width = parent_inverse.shape[-1]
    devices, struct = parent_pattern.shape
    unit = math.gcd(width, top_sigma.shape[0])
    groups = devices // struct
    if devices % struct == 0 and unit % (16 * groups) == 0:
        raw = exchange_two_hops(top_sigma, parent_pattern, width, unit, groups)
    else:
        raw = exchange_plain(top_sigma, parent_pattern, width)
    other_raw = swapped(raw, "row", 0)
    column, diagonal, both = parent_solve(raw, parent_panel, parent_inverse)
    other_both = swapped(both, "row", 0)
    child_col, child_diag = children_solve(
        other_raw, other_both, child_pattern, child_panel, child_inverse, child_count
    )
    return (column, diagonal, child_col, child_diag)


def solution(mesh):
    in_specs = (
        P(("hyper", "row"), None),
        P(),
        P(("hyper", "row"), None, None),
        P(("hyper", "row"), None, None),
        P("row", None),
        P(("hyper", "row"), None, None),
        P(("hyper", "row"), None, None),
        P("row"),
    )
    out_specs = (
        P(("hyper", "row"), None, None),
        P(("hyper", "row"), None, None),
        P(("hyper", "row"), None, None),
        P(("hyper", "row"), None, None),
    )
    return jax.shard_map(local, mesh=mesh, in_specs=in_specs, out_specs=out_specs, check_vma=False)
```

```python
import functools
import math

import jax
import jax.numpy as jnp
from jax import lax
from jax.experimental import pallas as pl
from jax.experimental.pallas import tpu as pltpu
from jax.sharding import PartitionSpec as P

BF16 = jnp.bfloat16
F32 = jnp.float32
VMEM_LIMIT = 40 * 2**20


def swapped(value, axis, distance):
    mask = 2**distance
    pairs = [(source, source ^ mask) for source in range(lax.axis_size(axis))]
    return lax.ppermute(value, axis, pairs)


def dot(a, b):
    return jnp.dot(a, b, preferred_element_type=F32)


def dot_t(a, b):
    return lax.dot_general(a, b, (((0,), (0,)), ((), ())), preferred_element_type=F32)


def from_top(per_parent, struct, super_, groups, cores, half, item, place, slot, pattern, top, out, sem):
    parent = item // per_parent
    row = (place[item] * cores + half) * groups
    for c in range(struct):
        column = pl.multiple_of(pattern[parent, c] * super_, super_)
        yield pltpu.make_async_copy(
            top.at[pl.ds(row, groups), :, pl.ds(column, super_)],
            out.at[:, c, slot[item]],
            sem,
        )


def give_kernel(items, sizes, core, place, slot, pattern, top, out, sem):
    def each(act):
        @pl.loop(0, items)
        def _(item):
            @pl.when(place[item] >= 0)
            def _():
                for copy in from_top(*sizes, 1 - core[0], item, place, slot, pattern, top, out, sem):
                    act(copy)

    each(lambda copy: copy.start())
    each(lambda copy: copy.wait())


def pack_kernel(items, sizes, core, place, slot, pattern, top, got, out, sem):
    def each(act):
        @pl.loop(0, items)
        def _(item):
            @pl.when(place[item] >= 0)
            def _():
                for copy in from_top(*sizes, core[0], item, place, slot, pattern, top, out, sem):
                    act(copy)

            @pl.when(place[item] == -1)
            def _():
                act(pltpu.make_async_copy(got.at[:, :, slot[item]], out.at[:, :, slot[item]], sem))

    each(lambda copy: copy.start())
    each(lambda copy: copy.wait())


def pick_kernel(items, per_parent, cores, chip, slot, held, out, sem):
    @pl.loop(0, items)
    def _(item):
        for core in range(cores):
            pltpu.make_async_copy(
                held.at[chip[item] * cores + core, slot[item]],
                out.at[item // per_parent, lax.rem(item, per_parent), core],
                sem,
            ).start()

    pltpu.make_async_copy(out, out, sem).wait()


def sigma_block(raw, a, c):
    groups, _, _, halves = raw.shape[:4]
    return jnp.concatenate(
        [raw[i, c, a, h] for h in range(halves) for i in range(groups)], axis=0
    )


def parent_kernel(raw, panel, inverse, column, diagonal, both):
    struct = raw.shape[1]
    width = inverse.shape[-1]
    total = inverse[0].astype(F32)
    for a in range(struct):
        product = jnp.zeros((width, width), F32)
        for c in range(struct):
            product += dot(sigma_block(raw, a, c), panel[0, pl.ds(c * width, width), :])
        col = (-product).astype(BF16)
        column[0, pl.ds(a * width, width), :] = col
        both[a] = col
        total -= dot_t(panel[0, pl.ds(a * width, width), :], col)
    diagonal[0] = total
    both[struct] = total.astype(BF16)


def child_kernel(positions, count, raw, both, panel, inverse, column, diagonal, sigma, beside_t):
    struct = raw.shape[1]
    width = inverse.shape[-1]
    picks = positions.shape[1]
    child = pl.program_id(0)

    @pl.when(child == 0)
    def _():
        for a in range(struct):
            for c in range(struct):
                sigma[a * struct + c] = sigma_block(raw, a, c)
            beside_t[a] = both[a].T

    @pl.when(child < count[0])
    def _():
        q = [positions[child, i] for i in range(picks)]
        parts = [panel[0, pl.ds(i * width, width), :] for i in range(picks + 1)]
        product = dot(both[struct], parts[0])
        for i in range(picks):
            product += dot(beside_t[q[i]], parts[1 + i])
        col = (-product).astype(BF16)
        column[0, pl.ds(0, width), :] = col
        total = inverse[0].astype(F32) - dot_t(parts[0], col)
        for i in range(picks):
            product = dot(both[q[i]], parts[0])
            for j in range(picks):
                product += dot(sigma[q[i] * struct + q[j]], parts[1 + j])
            col = (-product).astype(BF16)
            column[0, pl.ds((1 + i) * width, width), :] = col
            total -= dot_t(parts[1 + i], col)
        diagonal[0] = total

    @pl.when(child >= count[0])
    def _():
        column[...] = jnp.zeros_like(column)
        diagonal[...] = jnp.zeros_like(diagonal)


def parent_solve(raw, panel, inverse):
    struct, width = raw.shape[1], inverse.shape[-1]
    return pl.pallas_call(
        parent_kernel,
        out_shape=(
            jax.ShapeDtypeStruct((1, struct * width, width), BF16),
            jax.ShapeDtypeStruct((1, width, width), F32),
            jax.ShapeDtypeStruct((struct + 1, width, width), BF16),
        ),
        compiler_params=pltpu.CompilerParams(vmem_limit_bytes=VMEM_LIMIT),
        name="parent",
    )(raw, panel, inverse)


def children_solve(raw, both, positions, panel, inverse, count):
    kids, rows, width = panel.shape
    struct = raw.shape[1]

    def whole(shape):
        return pl.BlockSpec(shape, lambda k, *_: (0,) * len(shape))

    def one(shape):
        return pl.BlockSpec((1,) + shape, lambda k, *_: (k, 0, 0))

    return pl.pallas_call(
        child_kernel,
        grid_spec=pltpu.PrefetchScalarGridSpec(
            num_scalar_prefetch=2,
            grid=(kids,),
            in_specs=[whole(raw.shape), whole(both.shape), one((rows, width)), one((width, width))],
            out_specs=[one((rows, width)), one((width, width))],
            scratch_shapes=[
                pltpu.VMEM((struct * struct, width, width), BF16),
                pltpu.VMEM((struct, width, width), BF16),
            ],
        ),
        out_shape=(
            jax.ShapeDtypeStruct((kids, rows, width), BF16),
            jax.ShapeDtypeStruct((kids, width, width), F32),
        ),
        compiler_params=pltpu.CompilerParams(vmem_limit_bytes=VMEM_LIMIT),
        name="children",
    )(positions, count, raw, both, panel, inverse)


def exchange_plain(top_sigma, parent_pattern, width):
    devices = parent_pattern.shape[0]
    strip, total_rows = top_sigma.shape
    struct = parent_pattern.shape[1]
    blocks = total_rows // width
    picked = jnp.take(top_sigma.reshape(strip, blocks, width), parent_pattern, axis=1)
    outgoing = jnp.transpose(picked, (1, 0, 2, 3)).reshape(devices, strip, struct * width)
    arrived = lax.all_to_all(outgoing, "row", split_axis=0, concat_axis=1, tiled=True)
    columns = arrived[0].reshape(blocks, width, struct, width)
    mine = jnp.take(columns, parent_pattern[lax.axis_index("row")], axis=0)
    return jnp.transpose(mine, (2, 0, 1, 3))[None, :, :, None]


def schedule(parent_pattern, halves, own, cores):
    me = lax.axis_index("row")
    units = (parent_pattern[:, :, None] * halves + jnp.arange(halves, dtype=jnp.int32)).reshape(-1)
    chip = units // (own * cores)
    earlier = jnp.arange(units.size)[None, :] < jnp.arange(units.size)[:, None]
    slot = jnp.sum(
        jnp.logical_and(chip[None, :] == chip[:, None], earlier), axis=1, dtype=jnp.int32
    )
    offset = units - me * own
    mine = jnp.logical_and(offset >= 0, offset < own)
    place = jnp.where(mine, offset, jnp.where(chip == me // cores, -1, -2))
    return chip, place, slot


def exchange_two_hops(top_sigma, parent_pattern, width, unit, groups, cores):
    devices, struct = parent_pattern.shape
    halves, own = width // unit, top_sigma.shape[0] // unit
    per_parent = struct * halves
    items = devices * per_parent
    piece = unit // (groups * cores)
    chip, place, slot = schedule(parent_pattern, halves, own, cores)
    core = lax.rem(lax.axis_index("row"), cores).astype(jnp.int32)[None]
    most = devices * min(cores * own, per_parent)
    levels = [k for k in (18, 20, 21, 22, 23, 24, 25, 26, 28, 30, 33, 40, 56, 80) if k < most] + [most]
    strips = top_sigma.reshape(top_sigma.shape[0] // piece, piece, top_sigma.shape[1])
    smem = pl.BlockSpec(memory_space=pltpu.SMEM)
    hbm = pl.BlockSpec(memory_space=pl.ANY)
    vmem = pl.BlockSpec(memory_space=pltpu.VMEM)
    sizes = (per_parent, struct, width, groups, cores)
    params = pltpu.CompilerParams(vmem_limit_bytes=VMEM_LIMIT)

    def hop(slots, strips, core, chip, place, slot, pattern):
        shape = jax.ShapeDtypeStruct((groups, struct, slots, piece, width), BF16)
        give = pl.pallas_call(
            functools.partial(give_kernel, items, sizes),
            out_shape=shape,
            in_specs=[smem, smem, smem, smem, hbm],
            out_specs=vmem,
            scratch_shapes=[pltpu.SemaphoreType.DMA],
            compiler_params=params,
            name="give",
        )(core, place, slot, pattern, strips)
        got = swapped(give, "row", 0)
        outgoing = pl.pallas_call(
            functools.partial(pack_kernel, items, sizes),
            out_shape=shape,
            in_specs=[smem, smem, smem, smem, hbm, hbm],
            out_specs=vmem,
            scratch_shapes=[pltpu.SemaphoreType.DMA],
            compiler_params=params,
            name="pack",
        )(core, place, slot, pattern, strips, got)
        outgoing = outgoing.reshape(devices, slots, piece, width)
        held = lax.all_to_all(outgoing, "row", split_axis=0, concat_axis=0, tiled=True)
        return pl.pallas_call(
            functools.partial(pick_kernel, items, per_parent, cores),
            out_shape=jax.ShapeDtypeStruct((devices, per_parent, cores, piece, width), BF16),
            in_specs=[smem, smem, hbm],
            out_specs=hbm,
            scratch_shapes=[pltpu.SemaphoreType.DMA],
            name="pick",
        )(chip, slot, held)

    needed = jnp.max(slot) + 1
    level = jnp.sum(needed > jnp.array(levels[:-1], jnp.int32), dtype=jnp.int32)
    outgoing = lax.switch(
        level,
        [functools.partial(hop, slots) for slots in levels],
        strips, core, chip, place, slot, parent_pattern,
    )
    arrived = lax.all_to_all(outgoing, "row", split_axis=0, concat_axis=0, tiled=True)
    return arrived.reshape(groups, struct, struct, halves * cores, piece, width)


def local(
    top_sigma,
    parent_pattern,
    parent_panel,
    parent_inverse,
    child_pattern,
    child_panel,
    child_inverse,
    child_count,
):
    width = parent_inverse.shape[-1]
    devices, struct = parent_pattern.shape
    unit = math.gcd(width, top_sigma.shape[0])
    groups = devices // struct
    cores = 2
    if devices % (struct * cores) == 0 and unit % (16 * groups * cores) == 0:
        raw = exchange_two_hops(top_sigma, parent_pattern, width, unit, groups, cores)
    else:
        raw = exchange_plain(top_sigma, parent_pattern, width)
    other_raw = swapped(raw, "row", 0)
    column, diagonal, both = parent_solve(raw, parent_panel, parent_inverse)
    other_both = swapped(both, "row", 0)
    child_col, child_diag = children_solve(
        other_raw, other_both, child_pattern, child_panel, child_inverse, child_count
    )
    return (column, diagonal, child_col, child_diag)


def solution(mesh):
    in_specs = (
        P(("hyper", "row"), None),
        P(),
        P(("hyper", "row"), None, None),
        P(("hyper", "row"), None, None),
        P("row", None),
        P(("hyper", "row"), None, None),
        P(("hyper", "row"), None, None),
        P("row"),
    )
    out_specs = (
        P(("hyper", "row"), None, None),
        P(("hyper", "row"), None, None),
        P(("hyper", "row"), None, None),
        P(("hyper", "row"), None, None),
    )
    return jax.shard_map(local, mesh=mesh, in_specs=in_specs, out_specs=out_specs, check_vma=False)
```

```python
import functools
import math

import jax
import jax.numpy as jnp
from jax import lax
from jax.experimental import pallas as pl
from jax.experimental.pallas import tpu as pltpu
from jax.sharding import PartitionSpec as P

BF16 = jnp.bfloat16
F32 = jnp.float32
VMEM_LIMIT = 40 * 2**20


def swapped(value, axis, distance):
    mask = 2**distance
    pairs = [(source, source ^ mask) for source in range(lax.axis_size(axis))]
    return lax.ppermute(value, axis, pairs)


def dot(a, b):
    return jnp.dot(a, b, preferred_element_type=F32)


def dot_t(a, b):
    return lax.dot_general(a, b, (((0,), (0,)), ((), ())), preferred_element_type=F32)


def from_top(per_parent, struct, super_, groups, cores, half, item, place, slot, pattern, top, out, sem):
    parent = item // per_parent
    row = (place[item] * cores + half) * groups
    for c in range(struct):
        column = pl.multiple_of(pattern[parent, c] * super_, super_)
        yield pltpu.make_async_copy(
            top.at[pl.ds(row, groups), :, pl.ds(column, super_)],
            out.at[:, c, slot[item]],
            sem,
        )


def wait_units(number, out, sem):
    @pl.loop(0, number)
    def _(_):
        pltpu.make_async_copy(out.at[:, :, 0], out.at[:, :, 0], sem).wait()


def give_kernel(items, sizes, core, numbers, place, slot, pattern, top, out, sem):
    @pl.loop(0, items)
    def _(item):
        @pl.when(place[item] >= 0)
        def _():
            for copy in from_top(*sizes, 1 - core[0], item, place, slot, pattern, top, out, sem):
                copy.start()

    wait_units(numbers[0], out, sem)


def pack_kernel(items, sizes, core, numbers, place, slot, pattern, top, got, out, sem):
    @pl.loop(0, items)
    def _(item):
        @pl.when(place[item] >= 0)
        def _():
            for copy in from_top(*sizes, core[0], item, place, slot, pattern, top, out, sem):
                copy.start()

        @pl.when(place[item] == -1)
        def _():
            pltpu.make_async_copy(got.at[:, :, slot[item]], out.at[:, :, slot[item]], sem).start()

    wait_units(numbers[1], out, sem)


def pick_kernel(items, per_parent, cores, chip, slot, held, out, sem):
    @pl.loop(0, items)
    def _(item):
        for core in range(cores):
            pltpu.make_async_copy(
                held.at[chip[item] * cores + core, slot[item]],
                out.at[item // per_parent, lax.rem(item, per_parent), core],
                sem,
            ).start()

    pltpu.make_async_copy(out, out, sem).wait()


def sigma_block(raw, a, c):
    groups, _, _, halves = raw.shape[:4]
    return jnp.concatenate(
        [raw[i, c, a, h] for h in range(halves) for i in range(groups)], axis=0
    )


def parent_kernel(raw, panel, inverse, column, diagonal, both):
    struct = raw.shape[1]
    width = inverse.shape[-1]
    total = inverse[0].astype(F32)
    for a in range(struct):
        product = jnp.zeros((width, width), F32)
        for c in range(struct):
            product += dot(sigma_block(raw, a, c), panel[0, pl.ds(c * width, width), :])
        col = (-product).astype(BF16)
        column[0, pl.ds(a * width, width), :] = col
        both[a] = col
        total -= dot_t(panel[0, pl.ds(a * width, width), :], col)
    diagonal[0] = total
    both[struct] = total.astype(BF16)


def child_kernel(positions, count, raw, both, panel, inverse, column, diagonal, sigma, beside_t, matrix):
    struct = raw.shape[1]
    width = inverse.shape[-1]
    picks = positions.shape[1]
    child = pl.program_id(0)

    @pl.when(child == 0)
    def _():
        for a in range(struct):
            for c in range(struct):
                sigma[a * struct + c] = sigma_block(raw, a, c)
            beside_t[a] = both[a].T
        matrix[pl.ds(0, width), pl.ds(0, width)] = both[struct]

    @pl.when(child < count[0])
    def _():
        q = [positions[child, i] for i in range(picks)]
        at = [pl.ds((1 + i) * width, width) for i in range(picks)]
        for i in range(picks):
            matrix[pl.ds(0, width), at[i]] = beside_t[q[i]]
            matrix[at[i], pl.ds(0, width)] = both[q[i]]
            for j in range(picks):
                matrix[at[i], at[j]] = sigma[q[i] * struct + q[j]]
        col = (-dot(matrix[...], panel[0])).astype(BF16)
        column[0] = col
        diagonal[0] = inverse[0].astype(F32) - dot_t(panel[0], col)

    @pl.when(child >= count[0])
    def _():
        column[...] = jnp.zeros_like(column)
        diagonal[...] = jnp.zeros_like(diagonal)


def parent_solve(raw, panel, inverse):
    struct, width = raw.shape[1], inverse.shape[-1]
    return pl.pallas_call(
        parent_kernel,
        out_shape=(
            jax.ShapeDtypeStruct((1, struct * width, width), BF16),
            jax.ShapeDtypeStruct((1, width, width), F32),
            jax.ShapeDtypeStruct((struct + 1, width, width), BF16),
        ),
        compiler_params=pltpu.CompilerParams(vmem_limit_bytes=VMEM_LIMIT),
        name="parent",
    )(raw, panel, inverse)


def children_solve(raw, both, positions, panel, inverse, count):
    kids, rows, width = panel.shape
    struct = raw.shape[1]

    def whole(shape):
        return pl.BlockSpec(shape, lambda k, *_: (0,) * len(shape))

    def one(shape):
        return pl.BlockSpec((1,) + shape, lambda k, *_: (k, 0, 0))

    return pl.pallas_call(
        child_kernel,
        grid_spec=pltpu.PrefetchScalarGridSpec(
            num_scalar_prefetch=2,
            grid=(kids,),
            in_specs=[whole(raw.shape), whole(both.shape), one((rows, width)), one((width, width))],
            out_specs=[one((rows, width)), one((width, width))],
            scratch_shapes=[
                pltpu.VMEM((struct * struct, width, width), BF16),
                pltpu.VMEM((struct, width, width), BF16),
                pltpu.VMEM((rows, rows), BF16),
            ],
        ),
        out_shape=(
            jax.ShapeDtypeStruct((kids, rows, width), BF16),
            jax.ShapeDtypeStruct((kids, width, width), F32),
        ),
        compiler_params=pltpu.CompilerParams(vmem_limit_bytes=VMEM_LIMIT),
        name="children",
    )(positions, count, raw, both, panel, inverse)


def exchange_plain(top_sigma, parent_pattern, width):
    devices = parent_pattern.shape[0]
    strip, total_rows = top_sigma.shape
    struct = parent_pattern.shape[1]
    blocks = total_rows // width
    picked = jnp.take(top_sigma.reshape(strip, blocks, width), parent_pattern, axis=1)
    outgoing = jnp.transpose(picked, (1, 0, 2, 3)).reshape(devices, strip, struct * width)
    arrived = lax.all_to_all(outgoing, "row", split_axis=0, concat_axis=1, tiled=True)
    columns = arrived[0].reshape(blocks, width, struct, width)
    mine = jnp.take(columns, parent_pattern[lax.axis_index("row")], axis=0)
    return jnp.transpose(mine, (2, 0, 1, 3))[None, :, :, None]


def schedule(parent_pattern, halves, own, cores):
    me = lax.axis_index("row")
    units = (parent_pattern[:, :, None] * halves + jnp.arange(halves, dtype=jnp.int32)).reshape(-1)
    chip = units // (own * cores)
    earlier = jnp.arange(units.size)[None, :] < jnp.arange(units.size)[:, None]
    slot = jnp.sum(
        jnp.logical_and(chip[None, :] == chip[:, None], earlier), axis=1, dtype=jnp.int32
    )
    offset = units - me * own
    mine = jnp.logical_and(offset >= 0, offset < own)
    place = jnp.where(mine, offset, jnp.where(chip == me // cores, -1, -2))
    return chip, place, slot


def exchange_two_hops(top_sigma, parent_pattern, width, unit, groups, cores):
    devices, struct = parent_pattern.shape
    halves, own = width // unit, top_sigma.shape[0] // unit
    per_parent = struct * halves
    items = devices * per_parent
    piece = unit // (groups * cores)
    chip, place, slot = schedule(parent_pattern, halves, own, cores)
    core = lax.rem(lax.axis_index("row"), cores).astype(jnp.int32)[None]
    numbers = jnp.sum(place[None, :] >= jnp.array([[0], [-1]]), axis=1, dtype=jnp.int32)
    most = devices * min(cores * own, per_parent)
    levels = [k for k in (18, 20, 21, 22, 23, 24, 25, 26, 28, 30, 33, 40, 56, 80) if k < most] + [most]
    strips = top_sigma.reshape(top_sigma.shape[0] // piece, piece, top_sigma.shape[1])
    smem = pl.BlockSpec(memory_space=pltpu.SMEM)
    hbm = pl.BlockSpec(memory_space=pl.ANY)
    vmem = pl.BlockSpec(memory_space=pltpu.VMEM)
    sizes = (per_parent, struct, width, groups, cores)
    params = pltpu.CompilerParams(vmem_limit_bytes=VMEM_LIMIT)

    def hop(slots, strips, core, numbers, chip, place, slot, pattern):
        shape = jax.ShapeDtypeStruct((groups, struct, slots, piece, width), BF16)
        give = pl.pallas_call(
            functools.partial(give_kernel, items, sizes),
            out_shape=shape,
            in_specs=[smem, smem, smem, smem, smem, hbm],
            out_specs=vmem,
            scratch_shapes=[pltpu.SemaphoreType.DMA],
            compiler_params=params,
            name="give",
        )(core, numbers, place, slot, pattern, strips)
        got = swapped(give, "row", 0)
        outgoing = pl.pallas_call(
            functools.partial(pack_kernel, items, sizes),
            out_shape=shape,
            in_specs=[smem, smem, smem, smem, smem, hbm, hbm],
            out_specs=vmem,
            scratch_shapes=[pltpu.SemaphoreType.DMA],
            compiler_params=params,
            name="pack",
        )(core, numbers, place, slot, pattern, strips, got)
        outgoing = outgoing.reshape(devices, slots, piece, width)
        held = lax.all_to_all(outgoing, "row", split_axis=0, concat_axis=0, tiled=True)
        return pl.pallas_call(
            functools.partial(pick_kernel, items, per_parent, cores),
            out_shape=jax.ShapeDtypeStruct((devices, per_parent, cores, piece, width), BF16),
            in_specs=[smem, smem, hbm],
            out_specs=hbm,
            scratch_shapes=[pltpu.SemaphoreType.DMA],
            name="pick",
        )(chip, slot, held)

    needed = jnp.max(slot) + 1
    level = jnp.sum(needed > jnp.array(levels[:-1], jnp.int32), dtype=jnp.int32)
    outgoing = lax.switch(
        level,
        [functools.partial(hop, slots) for slots in levels],
        strips, core, numbers, chip, place, slot, parent_pattern,
    )
    arrived = lax.all_to_all(outgoing, "row", split_axis=0, concat_axis=0, tiled=True)
    return arrived.reshape(groups, struct, struct, halves * cores, piece, width)


def local(
    top_sigma,
    parent_pattern,
    parent_panel,
    parent_inverse,
    child_pattern,
    child_panel,
    child_inverse,
    child_count,
):
    width = parent_inverse.shape[-1]
    devices, struct = parent_pattern.shape
    unit = math.gcd(width, top_sigma.shape[0])
    groups = devices // struct
    cores = 2
    if devices % (struct * cores) == 0 and unit % (16 * groups * cores) == 0:
        raw = exchange_two_hops(top_sigma, parent_pattern, width, unit, groups, cores)
    else:
        raw = exchange_plain(top_sigma, parent_pattern, width)
    other_raw = swapped(raw, "row", 0)
    column, diagonal, both = parent_solve(raw, parent_panel, parent_inverse)
    other_both = swapped(both, "row", 0)
    child_col, child_diag = children_solve(
        other_raw, other_both, child_pattern, child_panel, child_inverse, child_count
    )
    return (column, diagonal, child_col, child_diag)


def solution(mesh):
    in_specs = (
        P(("hyper", "row"), None),
        P(),
        P(("hyper", "row"), None, None),
        P(("hyper", "row"), None, None),
        P("row", None),
        P(("hyper", "row"), None, None),
        P(("hyper", "row"), None, None),
        P("row"),
    )
    out_specs = (
        P(("hyper", "row"), None, None),
        P(("hyper", "row"), None, None),
        P(("hyper", "row"), None, None),
        P(("hyper", "row"), None, None),
    )
    return jax.shard_map(local, mesh=mesh, in_specs=in_specs, out_specs=out_specs, check_vma=False)
```

```python
import functools
import math

import jax
import jax.numpy as jnp
from jax import lax
from jax.experimental import pallas as pl
from jax.experimental.pallas import tpu as pltpu
from jax.sharding import PartitionSpec as P

BF16 = jnp.bfloat16
F32 = jnp.float32
VMEM_LIMIT = 40 * 2**20


def swapped(value, axis, distance):
    mask = 2**distance
    pairs = [(source, source ^ mask) for source in range(lax.axis_size(axis))]
    return lax.ppermute(value, axis, pairs)


def dot(a, b):
    return jnp.dot(a, b, preferred_element_type=F32)


def dot_t(a, b):
    return lax.dot_general(a, b, (((0,), (0,)), ((), ())), preferred_element_type=F32)


def from_top(per_parent, struct, super_, groups, cores, half, item, place, slot, pattern, top, out, sem):
    parent = item // per_parent
    row = (place[item] * cores + half) * groups
    for c in range(struct):
        column = pl.multiple_of(pattern[parent, c] * super_, super_)
        yield pltpu.make_async_copy(
            top.at[pl.ds(row, groups), :, pl.ds(column, super_)],
            out.at[:, c, slot[item]],
            sem,
        )


def wait_units(number, out, sem):
    @pl.loop(0, number)
    def _(_):
        pltpu.make_async_copy(out.at[:, :, 0], out.at[:, :, 0], sem).wait()


def give_kernel(items, sizes, core, numbers, place, slot, pattern, top, out, sem):
    @pl.loop(0, items, unroll=8)
    def _(item):
        @pl.when(place[item] >= 0)
        def _():
            for copy in from_top(*sizes, 1 - core[0], item, place, slot, pattern, top, out, sem):
                copy.start()

    wait_units(numbers[0], out, sem)


def pack_kernel(items, sizes, core, numbers, place, slot, pattern, top, got, out, sem):
    @pl.loop(0, items, unroll=8)
    def _(item):
        @pl.when(place[item] >= 0)
        def _():
            for copy in from_top(*sizes, core[0], item, place, slot, pattern, top, out, sem):
                copy.start()

        @pl.when(place[item] == -1)
        def _():
            pltpu.make_async_copy(got.at[:, :, slot[item]], out.at[:, :, slot[item]], sem).start()

    wait_units(numbers[1], out, sem)


def pick_kernel(items, per_parent, cores, chip, slot, held, out, sem):
    @pl.loop(0, items, unroll=8)
    def _(item):
        for core in range(cores):
            pltpu.make_async_copy(
                held.at[chip[item] * cores + core, slot[item]],
                out.at[item // per_parent, lax.rem(item, per_parent), core],
                sem,
            ).start()

    pltpu.make_async_copy(out, out, sem).wait()


def sigma_block(raw, a, c):
    groups, _, _, halves = raw.shape[:4]
    return jnp.concatenate(
        [raw[i, c, a, h] for h in range(halves) for i in range(groups)], axis=0
    )


def parent_kernel(raw, panel, inverse, column, diagonal, both):
    struct = raw.shape[1]
    width = inverse.shape[-1]
    total = inverse[0].astype(F32)
    for a in range(struct):
        product = jnp.zeros((width, width), F32)
        for c in range(struct):
            product += dot(sigma_block(raw, a, c), panel[0, pl.ds(c * width, width), :])
        col = (-product).astype(BF16)
        column[0, pl.ds(a * width, width), :] = col
        both[a] = col
        total -= dot_t(panel[0, pl.ds(a * width, width), :], col)
    diagonal[0] = total
    both[struct] = total.astype(BF16)


def child_kernel(positions, count, raw, both, panel, inverse, column, diagonal, sigma, beside_t, matrix):
    struct = raw.shape[1]
    width = inverse.shape[-1]
    picks = positions.shape[1]
    child = pl.program_id(0)

    @pl.when(child == 0)
    def _():
        for a in range(struct):
            for c in range(struct):
                sigma[a * struct + c] = sigma_block(raw, a, c)
            beside_t[a] = both[a].T
        matrix[pl.ds(0, width), pl.ds(0, width)] = both[struct]

    @pl.when(child < count[0])
    def _():
        q = [positions[child, i] for i in range(picks)]
        at = [pl.ds((1 + i) * width, width) for i in range(picks)]
        for i in range(picks):
            matrix[pl.ds(0, width), at[i]] = beside_t[q[i]]
            matrix[at[i], pl.ds(0, width)] = both[q[i]]
            for j in range(picks):
                matrix[at[i], at[j]] = sigma[q[i] * struct + q[j]]
        col = (-dot(matrix[...], panel[0])).astype(BF16)
        column[0] = col
        diagonal[0] = inverse[0].astype(F32) - dot_t(panel[0], col)

    @pl.when(child >= count[0])
    def _():
        column[...] = jnp.zeros_like(column)
        diagonal[...] = jnp.zeros_like(diagonal)


def parent_solve(raw, panel, inverse):
    struct, width = raw.shape[1], inverse.shape[-1]
    return pl.pallas_call(
        parent_kernel,
        out_shape=(
            jax.ShapeDtypeStruct((1, struct * width, width), BF16),
            jax.ShapeDtypeStruct((1, width, width), F32),
            jax.ShapeDtypeStruct((struct + 1, width, width), BF16),
        ),
        compiler_params=pltpu.CompilerParams(vmem_limit_bytes=VMEM_LIMIT),
        name="parent",
    )(raw, panel, inverse)


def children_solve(raw, both, positions, panel, inverse, count):
    kids, rows, width = panel.shape
    struct = raw.shape[1]

    def whole(shape):
        return pl.BlockSpec(shape, lambda k, *_: (0,) * len(shape))

    def one(shape):
        return pl.BlockSpec((1,) + shape, lambda k, *_: (k, 0, 0))

    return pl.pallas_call(
        child_kernel,
        grid_spec=pltpu.PrefetchScalarGridSpec(
            num_scalar_prefetch=2,
            grid=(kids,),
            in_specs=[whole(raw.shape), whole(both.shape), one((rows, width)), one((width, width))],
            out_specs=[one((rows, width)), one((width, width))],
            scratch_shapes=[
                pltpu.VMEM((struct * struct, width, width), BF16),
                pltpu.VMEM((struct, width, width), BF16),
                pltpu.VMEM((rows, rows), BF16),
            ],
        ),
        out_shape=(
            jax.ShapeDtypeStruct((kids, rows, width), BF16),
            jax.ShapeDtypeStruct((kids, width, width), F32),
        ),
        compiler_params=pltpu.CompilerParams(vmem_limit_bytes=VMEM_LIMIT),
        name="children",
    )(positions, count, raw, both, panel, inverse)


def exchange_plain(top_sigma, parent_pattern, width):
    devices = parent_pattern.shape[0]
    strip, total_rows = top_sigma.shape
    struct = parent_pattern.shape[1]
    blocks = total_rows // width
    picked = jnp.take(top_sigma.reshape(strip, blocks, width), parent_pattern, axis=1)
    outgoing = jnp.transpose(picked, (1, 0, 2, 3)).reshape(devices, strip, struct * width)
    arrived = lax.all_to_all(outgoing, "row", split_axis=0, concat_axis=1, tiled=True)
    columns = arrived[0].reshape(blocks, width, struct, width)
    mine = jnp.take(columns, parent_pattern[lax.axis_index("row")], axis=0)
    return jnp.transpose(mine, (2, 0, 1, 3))[None, :, :, None]


def schedule(parent_pattern, halves, own, cores):
    me = lax.axis_index("row")
    units = (parent_pattern[:, :, None] * halves + jnp.arange(halves, dtype=jnp.int32)).reshape(-1)
    chip = units // (own * cores)
    earlier = jnp.arange(units.size)[None, :] < jnp.arange(units.size)[:, None]
    slot = jnp.sum(
        jnp.logical_and(chip[None, :] == chip[:, None], earlier), axis=1, dtype=jnp.int32
    )
    offset = units - me * own
    mine = jnp.logical_and(offset >= 0, offset < own)
    place = jnp.where(mine, offset, jnp.where(chip == me // cores, -1, -2))
    return chip, place, slot


def exchange_two_hops(top_sigma, parent_pattern, width, unit, groups, cores):
    devices, struct = parent_pattern.shape
    halves, own = width // unit, top_sigma.shape[0] // unit
    per_parent = struct * halves
    items = devices * per_parent
    piece = unit // (groups * cores)
    chip, place, slot = schedule(parent_pattern, halves, own, cores)
    core = lax.rem(lax.axis_index("row"), cores).astype(jnp.int32)[None]
    numbers = jnp.sum(place[None, :] >= jnp.array([[0], [-1]]), axis=1, dtype=jnp.int32)
    most = devices * min(cores * own, per_parent)
    levels = [k for k in (18, 20, 21, 22, 23, 24, 25, 26, 28, 30, 33, 40, 56, 80) if k < most] + [most]
    strips = top_sigma.reshape(top_sigma.shape[0] // piece, piece, top_sigma.shape[1])
    smem = pl.BlockSpec(memory_space=pltpu.SMEM)
    hbm = pl.BlockSpec(memory_space=pl.ANY)
    vmem = pl.BlockSpec(memory_space=pltpu.VMEM)
    sizes = (per_parent, struct, width, groups, cores)
    params = pltpu.CompilerParams(vmem_limit_bytes=VMEM_LIMIT)

    def hop(slots, strips, core, numbers, chip, place, slot, pattern):
        shape = jax.ShapeDtypeStruct((groups, struct, slots, piece, width), BF16)
        give = pl.pallas_call(
            functools.partial(give_kernel, items, sizes),
            out_shape=shape,
            in_specs=[smem, smem, smem, smem, smem, hbm],
            out_specs=vmem,
            scratch_shapes=[pltpu.SemaphoreType.DMA],
            compiler_params=params,
            name="give",
        )(core, numbers, place, slot, pattern, strips)
        got = swapped(give, "row", 0)
        outgoing = pl.pallas_call(
            functools.partial(pack_kernel, items, sizes),
            out_shape=shape,
            in_specs=[smem, smem, smem, smem, smem, hbm, hbm],
            out_specs=vmem,
            scratch_shapes=[pltpu.SemaphoreType.DMA],
            compiler_params=params,
            name="pack",
        )(core, numbers, place, slot, pattern, strips, got)
        outgoing = outgoing.reshape(devices, slots, piece, width)
        held = lax.all_to_all(outgoing, "row", split_axis=0, concat_axis=0, tiled=True)
        return pl.pallas_call(
            functools.partial(pick_kernel, items, per_parent, cores),
            out_shape=jax.ShapeDtypeStruct((devices, per_parent, cores, piece, width), BF16),
            in_specs=[smem, smem, hbm],
            out_specs=hbm,
            scratch_shapes=[pltpu.SemaphoreType.DMA],
            name="pick",
        )(chip, slot, held)

    needed = jnp.max(slot) + 1
    level = jnp.sum(needed > jnp.array(levels[:-1], jnp.int32), dtype=jnp.int32)
    outgoing = lax.switch(
        level,
        [functools.partial(hop, slots) for slots in levels],
        strips, core, numbers, chip, place, slot, parent_pattern,
    )
    arrived = lax.all_to_all(outgoing, "row", split_axis=0, concat_axis=0, tiled=True)
    return arrived.reshape(groups, struct, struct, halves * cores, piece, width)


def local(
    top_sigma,
    parent_pattern,
    parent_panel,
    parent_inverse,
    child_pattern,
    child_panel,
    child_inverse,
    child_count,
):
    width = parent_inverse.shape[-1]
    devices, struct = parent_pattern.shape
    unit = math.gcd(width, top_sigma.shape[0])
    groups = devices // struct
    cores = 2
    if devices % (struct * cores) == 0 and unit % (16 * groups * cores) == 0:
        raw = exchange_two_hops(top_sigma, parent_pattern, width, unit, groups, cores)
    else:
        raw = exchange_plain(top_sigma, parent_pattern, width)
    other_raw = swapped(raw, "row", 0)
    column, diagonal, both = parent_solve(raw, parent_panel, parent_inverse)
    other_both = swapped(both, "row", 0)
    child_col, child_diag = children_solve(
        other_raw, other_both, child_pattern, child_panel, child_inverse, child_count
    )
    return (column, diagonal, child_col, child_diag)


def solution(mesh):
    in_specs = (
        P(("hyper", "row"), None),
        P(),
        P(("hyper", "row"), None, None),
        P(("hyper", "row"), None, None),
        P("row", None),
        P(("hyper", "row"), None, None),
        P(("hyper", "row"), None, None),
        P("row"),
    )
    out_specs = (
        P(("hyper", "row"), None, None),
        P(("hyper", "row"), None, None),
        P(("hyper", "row"), None, None),
        P(("hyper", "row"), None, None),
    )
    return jax.shard_map(local, mesh=mesh, in_specs=in_specs, out_specs=out_specs, check_vma=False)
```
